256 devices in a mesh: dp: 8 (over z_lo, core), expert: 32 (over z_hi, y, x).
Axes of the slice: x: 4, y: 4, z: 8 (z_hi: 2, z_lo: 4; z = z_hi * 4 + z_lo), core: 2. Of those that a mesh axis runs over, the one named last changes fastest.
Arguments:
- tokens: bfloat16 [65536, 1280], P(('dp', 'expert')), may hold values from -24 to 24
- router: bfloat16 [1280, 64], replicated, may hold values from -11 to 11
- w_in: bfloat16 [64, 1280, 4096], P('expert', None, 'dp'), may hold values from -0.15625 to 0.15625
- w_out: bfloat16 [64, 4096, 1280], P('expert', 'dp'), may hold values from -0.09375 to 0.09375
- out_grad: bfloat16 [65536, 1280], P(('dp', 'expert')), may hold values from -6 to 6
Outputs:
- token_grad: bfloat16 [65536, 1280], P(('dp', 'expert'))
- router_grad: float32 [1280, 64], replicated
- w_in_grad: bfloat16 [64, 1280, 4096], P('expert', None, 'dp')
- w_out_grad: bfloat16 [64, 4096, 1280], P('expert', 'dp')
The draws below stay inside these ranges and needn't reach their ends.
All inputs are finite; a program needn't handle non-finite values.
Results may differ from the reference program's by a relative error of at most 0.012.
Values may be sent and summed in bfloat16 or wider, within the bound.
A program may use at most 64 MiB of HBM per device.

```python
import math
import jax
import jax.numpy as jnp
from jax import lax

D = 1280
FF = 4096
M = 256
EXPERTS = 64
TOKENS = 65536


def draw_router(key, part):
    values = jax.random.truncated_normal(key, -4.0, 4.0, (D, EXPERTS), jnp.float32) / math.sqrt(D)
    return jnp.clip(values, -11.0, 11.0).astype(jnp.bfloat16)


def spiked(array, own_key, source, target, parts, factor):
    owner, partner = [(jnp.arange(array.shape[position]) // (array.shape[position] // parts)).reshape([-1 if axis == position else 1 for axis in range(array.ndim)]) for position in (source, target)]
    chosen = jax.random.permutation(own_key, parts)[partner]
    strong = (owner == chosen) | (owner == (partner + parts // 2) % parts)
    return jnp.where(strong, factor * array, array)


def block_scale(stream_key, dims, split, low, top_value):
    level, own = 1.0, jax.random.fold_in(stream_key, 6)
    for position, shards_of in split:
        steps = jnp.exp(jax.random.uniform(jax.random.fold_in(own, position), (shards_of,), jnp.float32, low / len(split), top_value / len(split)))
        level = level * jnp.repeat(steps, dims[position] // shards_of).reshape([-1 if axis == position else 1 for axis in range(len(dims))])
    return level


def bell_draw(stream_key, extent, scale, bound, split=(), kind=jnp.bfloat16):
    result = jax.random.normal(stream_key, extent, jnp.float32) * scale
    if len(split) > 0:
        result = block_scale(stream_key, extent, split, -0.22, 0.18) * result
    return jnp.clip(result, min=-bound, max=bound).astype(kind)


def noise_with(stream_key, extent, deviation, bound, pieces, heavy, kind=jnp.bfloat16):
    drawn = deviation * jax.random.normal(stream_key, extent, jnp.float32)
    if pieces:
        drawn = drawn * block_scale(stream_key, extent, pieces, -0.22, 0.18)
    return jnp.clip(spiked(drawn, jax.random.fold_in(stream_key, 3), *heavy), -bound, bound).astype(kind)


def setup_inputs(seed: int = 0) -> dict:
    arg_keys = jax.random.split(jax.random.key(seed), 6)
    tokens = noise_with(arg_keys[0], (TOKENS, D), 1.0, 24.0, ((0, 256),), (0, 1, 256, 6.0))
    router = draw_router(jax.random.fold_in(arg_keys[5], 71), 0)
    w_in = bell_draw(arg_keys[2], (EXPERTS, D, FF), D ** -0.5, 0.15625, ((0, 32), (2, 8)))
    w_out = bell_draw(arg_keys[3], (EXPERTS, FF, D), FF ** -0.5, 0.09375, ((0, 32), (1, 8)))
    out_grad = bell_draw(arg_keys[4], (TOKENS, D), 1.0, 6.0, ((0, 256),))
    return dict(tokens=tokens, router=router, w_in=w_in, w_out=w_out, out_grad=out_grad)


def activate(values):
    return jax.nn.gelu(values, approximate=True)

def expert_pass(operands):
    first, second, slot_in, slot_grad = operands
    hidden = jnp.dot(slot_in, first, preferred_element_type=jnp.float32)
    active, pull = jax.vjp(activate, hidden)
    active_b = active.astype(jnp.bfloat16)
    slot_out = jnp.dot(active_b, second, preferred_element_type=jnp.float32).astype(jnp.bfloat16)
    active_grad = lax.dot_general(slot_grad, second, (((1,), (1,)), ((), ())), preferred_element_type=jnp.float32)
    second_grad = lax.dot_general(active_b, slot_grad, (((0,), (0,)), ((), ())), preferred_element_type=jnp.float32).astype(jnp.bfloat16)
    hidden_grad = pull(active_grad)[0].astype(jnp.bfloat16)
    first_grad = lax.dot_general(slot_in, hidden_grad, (((0,), (0,)), ((), ())), preferred_element_type=jnp.float32).astype(jnp.bfloat16)
    input_grad = lax.dot_general(hidden_grad, first, (((1,), (1,)), ((), ())), preferred_element_type=jnp.float32).astype(jnp.bfloat16)
    return (slot_out, input_grad, first_grad, second_grad)

def reference(tokens, router, w_in, w_out, out_grad):
    images = tokens.shape[0] // M
    inputs = tokens.reshape(images, M, D).astype(jnp.float32)
    grads = out_grad.reshape(images, M, D).astype(jnp.float32)
    router_f = router.astype(jnp.float32)
    logits = jnp.einsum('bmd,de->bme', inputs, router_f)
    dispatch = jax.nn.softmax(logits, axis=1)
    combine = jax.nn.softmax(logits, axis=2)
    dispatch_b = dispatch.astype(jnp.bfloat16).astype(jnp.float32)
    combine_b = combine.astype(jnp.bfloat16).astype(jnp.float32)
    slots = jnp.einsum('bme,bmd->bed', dispatch_b, inputs).astype(jnp.bfloat16)
    slot_grad = jnp.einsum('bme,bmd->bed', combine_b, grads).astype(jnp.bfloat16)
    slot_out, slot_in_grad, first_grad, second_grad = lax.map(expert_pass, (w_in, w_out, jnp.swapaxes(slots, 0, 1), jnp.swapaxes(slot_grad, 0, 1)))
    slot_out = jnp.swapaxes(slot_out, 0, 1).astype(jnp.float32)
    slot_in_grad = jnp.swapaxes(slot_in_grad, 0, 1).astype(jnp.float32)
    combine_grad = jnp.einsum('bmd,bed->bme', grads, slot_out)
    dispatch_grad = jnp.einsum('bmd,bed->bme', inputs, slot_in_grad)
    logit_grad = combine * (combine_grad - lax.optimization_barrier(jnp.sum(combine_grad * combine, axis=2, keepdims=True)))
    logit_grad = logit_grad + dispatch * (dispatch_grad - lax.optimization_barrier(jnp.sum(dispatch_grad * dispatch, axis=1, keepdims=True)))
    logit_b = logit_grad.astype(jnp.bfloat16).astype(jnp.float32)
    token_grad = jnp.einsum('bme,bed->bmd', dispatch_b, slot_in_grad) + jnp.einsum('bme,de->bmd', logit_b, router_f)
    router_grad = jnp.einsum('bmd,bme->de', inputs, logit_b)
    return (token_grad.astype(jnp.bfloat16).reshape(images * M, D), router_grad, first_grad, second_grad)
```

```python
import math

import jax
import jax.numpy as jnp
from jax import lax
from jax.experimental import pallas as pl
from jax.experimental.pallas import tpu as pltpu
from jax.sharding import PartitionSpec as P

MESH = pl.DeviceIdType.MESH
M, D, E, FS = 256, 1280, 64, 512
BF, F32 = jnp.bfloat16, jnp.float32
GELU_C, GELU_A = math.sqrt(2.0 / math.pi), 0.044715


def dot(a, b, ca=1, cb=0):
    return lax.dot_general(a, b, (((ca,), (cb,)), ((), ())), preferred_element_type=F32)


def perm(source, inverse):
    rows = lax.broadcasted_iota(jnp.int32, (128, 128), 1 if inverse else 0)
    cols = lax.broadcasted_iota(jnp.int32, (128, 128), 0 if inverse else 1)
    return (source(rows) == cols).astype(F32).astype(BF)


def reorder(matrix, rows):
    return dot(matrix, rows).astype(BF)


def kernel(
    x_ref, g_ref, r_ref, wi_hbm, wo_hbm,
    tg_ref, rg_ref, wig_hbm, wog_hbm,
    wi, wo, wig, wog,
    comb_v, disp_v,
    zs, zr, sv, rv, ob, relay, rows, act, hgv,
    p32, cs, cr, pv, ru, rd, fo, rl, zs2, zr2, sv2, rv2,
    ra, rb, rc, rp, zb, rf,
    wsem, osem, core_s, core_r, xs1, xr1, xs2, xr2,
    gr, gsu, gsd, gcs, gcr, pcs, pcr,
    rur, rdr, fr, rsu, rsd, as1, ar1, az_s, az_r, as2, ar2,
):
    dp, ex = lax.axis_index("dp"), lax.axis_index("expert")
    c, q = dp % 2, dp // 2
    h, xy = ex // 16, ex % 16
    y, x = xy // 4, xy % 4

    core_peer = (q * 2 + (1 - c), ex)
    xy_peers = []
    for d in range(1, 16):
        to = ((y + d // 4) % 4) * 4 + (x + d % 4) % 4
        frm = ((y + 4 - d // 4) % 4) * 4 + (x + 4 - d % 4) % 4
        xy_peers.append((d, to, frm))

    def z_dev(hh, qq):
        return (qq * 2 + c, hh * 16 + xy)

    barrier = pltpu.get_barrier_semaphore()

    def greet(dev):
        pl.semaphore_signal(barrier, inc=1, device_id=dev, device_id_type=MESH)

    greet(core_peer)
    for d, to, frm in xy_peers:
        greet((dp, h * 16 + to))
    z = h * 4 + q
    z_peers = []
    for d in range(1, 8):
        zt, zf = (z + d) % 8, (z + 8 - d) % 8
        z_peers.append((d, (zt % 4 * 2 + c, zt // 4 * 16 + xy), zf))
        greet(z_peers[-1][1])

    def remote(src, dst, ss, rs, dev):
        return pltpu.make_async_remote_copy(
            src_ref=src, dst_ref=dst, send_sem=ss, recv_sem=rs, device_id=dev, device_id_type=MESH
        )

    w_in_copy = pltpu.make_async_copy(wi_hbm, wi, wsem.at[0])
    w_out_copy = pltpu.make_async_copy(wo_hbm, wo, wsem.at[1])
    w_in_copy.start()
    w_out_copy.start()

    logits = dot(x_ref[...], r_ref[...])
    ed = jnp.exp(logits - jnp.max(logits, axis=0, keepdims=True))
    dispatch = ed / jnp.sum(ed, axis=0, keepdims=True)
    ec = jnp.exp(logits - jnp.max(logits, axis=1, keepdims=True))
    combine = ec / jnp.sum(ec, axis=1, keepdims=True)
    disp_v[...] = dispatch
    comb_v[...] = combine
    slots = dot(dispatch.astype(BF), x_ref[...], 0, 0).astype(BF)
    grads = dot(combine.astype(BF), g_ref[...], 0, 0).astype(BF)

    def order1(r):
        parity = jnp.where(r < 64, c, 1 - c)
        return ((r >> 5) & 1) * 64 + (r & 31) * 2 + parity

    def order2(r):
        half = jnp.where(((r >> 2) & 1) == 0, h, 1 - h)
        return (r & 1) * 64 + ((r >> 1) & 1) * 32 + half * 16 + (r >> 3)

    def order3(r):
        return ((r >> 1) & 15) * 8 + (r >> 5) * 2 + (r & 1)

    z1 = reorder(perm(order1, False), jnp.concatenate([slots, grads], axis=0))
    zs[...] = z1.reshape(2, 64, D)

    pl.semaphore_wait(barrier, 23)

    swap = remote(zs.at[1], zr, core_s.at[0], core_r.at[0], core_peer)
    swap.start()
    swap.wait()
    s1 = reorder(perm(order2, False), jnp.concatenate([zs[0], zr[...]], axis=0))
    sv[...] = s1.reshape(16, 8, D)

    def plane_exchange(src, dst, ss, rs):
        copies = []
        for d, to, frm in xy_peers:
            cp = remote(src.at[to], dst.at[xy], ss.at[d], rs.at[d], (dp, h * 16 + to))
            cp.start()
            copies.append(cp)
        dst[xy] = src[xy]
        return copies

    def finish(copies):
        for cp in copies:
            cp.wait()

    finish(plane_exchange(sv, rv, xs1, xr1))
    b1 = reorder(perm(order3, False), rv[...].reshape(128, D)).reshape(2, 2, 32, D)
    own = rows.at[1]
    for t in range(2):
        rows[1, t, q] = b1[0, t]
        ob[t] = b1[1, t]

    def g_copy(src, dst_idx, up, idx, qq):
        if up:
            dev = z_dev(h, qq + 1) if qq < 3 else z_dev(1 - h, 0)
        else:
            dev = z_dev(h, qq - 1) if qq > 0 else z_dev(1 - h, 3)
        dst = relay if dst_idx == 8 else own.at[:, dst_idx]
        sem = (gsu if up else gsd).at[idx]
        return remote(src, dst, sem, gr.at[dst_idx], dev)

    def g_recv(idx):
        dst = relay if idx == 8 else own.at[:, idx]
        remote(dst, dst, gsu.at[0], gr.at[idx], core_peer).wait_recv()

    def to_core(idx):
        return remote(own.at[:, idx], rows.at[0, :, idx], gcs.at[idx], gcr.at[idx], core_peer)

    def gather(qq, begin, events, last):
        sent = []

        def send(kind, up):
            if kind == "own":
                cp = g_copy(own.at[:, qq], qq, up, qq, qq)
            elif kind == "out":
                edge = (qq == 3 and up) or (qq == 0 and not up)
                cp = g_copy(ob, 4 + qq if edge else 8, up, 8, qq)
            elif kind == "relay":
                cp = g_copy(relay, 5 if qq == 0 else 6, up, 8 if qq == 3 else 7, qq)
            else:
                cp = g_copy(own.at[:, kind], kind, up, kind, qq)
            cp.start()
            sent.append(cp)

        for kind, up in begin:
            send(kind, up)
        cc = [to_core(qq)]
        cc[0].start()
        for idx, up in events:
            g_recv(idx)
            if up is not None:
                send("relay" if idx == 8 else idx, up)
            if idx != 8:
                cp = to_core(idx)
                cp.start()
                cc.append(cp)
        for cp in sent:
            cp.wait_send()
        for cp in cc:
            cp.wait()

    U, DN = True, False

    @pl.when(q == 0)
    def _():
        gather(0, [("own", U), ("out", DN)],
               [(7, U), (8, DN), (6, U), (1, None), (2, None), (3, None), (4, None), (5, None)], None)

    @pl.when(q == 1)
    def _():
        gather(1, [("out", DN), ("own", U), ("own", DN)],
               [(0, U), (2, DN), (7, U), (3, DN), (6, U), (4, DN), (5, DN)], None)

    @pl.when(q == 2)
    def _():
        gather(2, [("out", U), ("own", DN), ("own", U)],
               [(3, DN), (1, U), (4, DN), (0, U), (5, DN), (7, U), (6, U)], None)

    @pl.when(q == 3)
    def _():
        gather(3, [("own", DN), ("out", U)],
               [(4, DN), (8, U), (5, DN), (2, None), (1, None), (0, None), (7, None), (6, None)], None)

    w_in_copy.wait()
    w_out_copy.wait()

    def core_sum(t):
        return remote(cs.at[t], cr.at[t], pcs.at[t], pcr.at[t], core_peer)

    def expert(s, _):
        e = jnp.where(s == 1, c, 1 - c)
        hidden = dot(rows[s, 0].reshape(M, D), wi[e])
        inner = jnp.tanh(GELU_C * (hidden + GELU_A * hidden * hidden * hidden))
        cdf = 0.5 * (1.0 + inner)
        slope = cdf + hidden * (
            0.5 * (1.0 - inner * inner) * (GELU_C * (1.0 + 3.0 * GELU_A * hidden * hidden))
        )
        active = (hidden * cdf).astype(BF)
        act[s] = active
        out = dot(active, wo[e])

        @pl.when(s == 0)
        def _():
            cs[0] = out.astype(BF).reshape(8, 32, D)
            core_sum(0).start()

        @pl.when(s == 1)
        def _():
            p32[0] = out

        hg = (dot(rows[s, 1].reshape(M, D), wo[e], 1, 1) * slope).astype(BF)
        hgv[s] = hg
        back = dot(hg, wi[e], 1, 1)

        @pl.when(s == 0)
        def _():
            cs[1] = back.astype(BF).reshape(8, 32, D)
            core_sum(1).start()

        @pl.when(s == 1)
        def _():
            p32[1] = back

        return 0

    lax.fori_loop(0, 2, expert, 0)
    for t in range(2):
        core_sum(t).wait()
        pv[t] = (p32[t] + cr[t].reshape(M, D).astype(F32)).astype(BF).reshape(8, 32, D)

    def weight_grads(s, _):
        e = jnp.where(s == 1, c, 1 - c)
        wog[e] = dot(act[s], rows[s, 1].reshape(M, D), 0, 0).astype(BF)
        wig[e] = dot(rows[s, 0].reshape(M, D), hgv[s], 0, 0).astype(BF)
        return 0

    out_copies = [
        pltpu.make_async_copy(wig, wig_hbm, osem.at[0]),
        pltpu.make_async_copy(wog, wog_hbm, osem.at[1]),
    ]

    def r_dev(up, qq):
        if up:
            return z_dev(h, qq + 1) if qq < 3 else z_dev(1 - h, 0)
        return z_dev(h, qq - 1) if qq > 0 else z_dev(1 - h, 3)

    def r_copy(src, up, idx, qq):
        ss = (rsu if up else rsd).at[idx]
        dev = r_dev(up, qq)
        if idx == 8:
            return remote(src, fo, ss, fr.at[0], dev)
        if up and qq == 3 or not up and qq == 0:
            if idx in (4, 7):
                return remote(src, fo, ss, fr.at[0], dev)
            return remote(src, rl, ss, fr.at[1], dev)
        dst, rs = (ru, rur) if up else (rd, rdr)
        return remote(src, dst.at[:, idx], ss, rs.at[idx], dev)

    def r_wait(up, idx):
        dst, rs = (ru, rur) if up else (rd, rdr)
        remote(dst.at[:, idx], dst.at[:, idx], rsu.at[0], rs.at[idx], core_peer).wait_recv()

    def f_wait(k):
        dst = (fo, rl)[k]
        remote(dst, dst, rsu.at[0], fr.at[k], core_peer).wait_recv()

    def begin_reduce(qq):
        up = qq == 0
        for idx in (5, 4, 3, 2, 1) if up else (6, 7, 0, 1, 2):
            r_copy(pv.at[:, idx], up, idx, qq).start()

    def step(qq, up, idx):
        r_wait(up, idx)
        dst = ru if up else rd
        dst[:, idx] = (dst[:, idx].astype(F32) + pv[:, idx].astype(F32)).astype(BF)
        r_copy(dst.at[:, idx], up, idx, qq).start()

    @pl.when(q == 0)
    def _():
        begin_reduce(0)

    @pl.when(q == 3)
    def _():
        begin_reduce(3)

    def finish_reduce(qq, events):
        for up, idx in events:
            step(qq, up, idx)
        if qq in (0, 3):
            f_wait(1)
            r_copy(rl, qq == 0, 8, qq).start()
        total = pv[:, qq].astype(F32)
        if qq > 0:
            r_wait(True, qq)
            total = total + ru[:, qq].astype(F32)
        if qq < 3:
            r_wait(False, qq)
            total = total + rd[:, qq].astype(F32)
        f_wait(0)
        both = jnp.concatenate([total.astype(BF).reshape(64, D), fo[...].reshape(64, D)], axis=0)
        sv2[...] = reorder(perm(order3, True), both).reshape(16, 8, D)
        if qq in (0, 3):
            up = qq == 0
            for idx in (5, 4, 3, 2, 1) if up else (6, 7, 0, 1, 2):
                r_copy(pv.at[:, idx], up, idx, qq).wait_send()
            r_copy(rl, up, 8, qq).wait_send()
        for up, idx in events:
            dst = ru if up else rd
            r_copy(dst.at[:, idx], up, idx, qq).wait_send()

    @pl.when(q == 0)
    def _():
        finish_reduce(0, [(DN, 6), (DN, 7)])

    @pl.when(q == 1)
    def _():
        finish_reduce(1, [(U, 5), (DN, 6), (U, 4), (DN, 7), (U, 3), (DN, 0), (U, 2)])

    @pl.when(q == 2)
    def _():
        finish_reduce(2, [(DN, 6), (U, 5), (DN, 7), (U, 4), (DN, 0), (U, 3), (DN, 1)])

    @pl.when(q == 3)
    def _():
        finish_reduce(3, [(U, 5), (U, 4)])

    back_copies = plane_exchange(sv2, rv2, xs2, xr2)
    lax.fori_loop(0, 2, weight_grads, 0)
    for cp in out_copies:
        cp.start()
    finish(back_copies)
    zs2[...] = reorder(perm(order2, True), rv2[...].reshape(128, D)).reshape(2, 64, D)
    swap2 = remote(zs2.at[1], zr2, core_s.at[1], core_r.at[1], core_peer)
    swap2.start()
    swap2.wait()
    mine = reorder(perm(order1, True), jnp.concatenate([zs2[0], zr2[...]], axis=0))
    slot_out, slot_in = mine[:64], mine[64:]

    cg = dot(g_ref[...], slot_out, 1, 1)
    dg = dot(x_ref[...], slot_in, 1, 1)
    combine, dispatch = comb_v[...], disp_v[...]
    lg = combine * (cg - jnp.sum(cg * combine, axis=1, keepdims=True))
    lg = lg + dispatch * (dg - jnp.sum(dg * dispatch, axis=0, keepdims=True))
    lb = lg.astype(BF)
    part = dot(lb, x_ref[...], 0, 0)
    for p in range(16):
        ra[p] = part[p // 2 * 8 : p // 2 * 8 + 8, p % 2 * 640 : p % 2 * 640 + 640]
    copies = plane_exchange(ra, rb, as1, ar1)
    tg_ref[...] = (dot(dispatch.astype(BF), slot_in) + dot(lb, r_ref[...], 1, 1)).astype(BF)
    finish(copies)
    total = rb[0]
    for p in range(1, 16):
        total = total + rb[p]
    rp[0] = total
    swap3 = remote(rp.at[0], rp.at[1], core_s.at[2], core_r.at[2], core_peer)
    swap3.start()
    swap3.wait()
    zb[z] = rp[0] + rp[1]
    copies = []
    for d, dev, frm in z_peers:
        cp = remote(zb.at[z], zb.at[z], az_s.at[d], az_r.at[d], dev)
        cp.start()
        copies.append(cp)
    for (d, dev, frm), cp in zip(z_peers, copies):
        cp.wait_send()
        remote(zb.at[frm], zb.at[frm], az_s.at[d], az_r.at[d], dev).wait_recv()
    total = zb[0]
    for p in range(1, 8):
        total = total + zb[p]
    rf[...] = total
    rc[xy] = total
    copies = []
    for d, to, frm in xy_peers:
        cp = remote(rf, rc.at[xy], as2.at[d], ar2.at[d], (dp, h * 16 + to))
        cp.start()
        copies.append(cp)
    finish(copies)
    for p in range(8):
        rg_ref[p * 8 : p * 8 + 8, :640] = rc[2 * p]
        rg_ref[p * 8 : p * 8 + 8, 640:] = rc[2 * p + 1]
    for cp in out_copies:
        cp.wait()


def local(tokens, router, w_in, w_out, out_grad):
    vm = pl.BlockSpec(memory_space=pltpu.VMEM)
    anyspace = pl.BlockSpec(memory_space=pl.ANY)
    sem = pltpu.SemaphoreType.DMA
    v = pltpu.VMEM
    block = (2, 32, D)
    scratch = [
        v((2, D, FS), BF), v((2, FS, D), BF), v((2, D, FS), BF), v((2, FS, D), BF),
        v((M, E), F32), v((M, E), F32),
        v((2, 64, D), BF), v((64, D), BF), v((16, 8, D), BF), v((16, 8, D), BF),
        v(block, BF), v(block, BF), v((2, 2, 8, 32, D), BF), v((2, M, FS), BF), v((2, M, FS), BF),
        v((2, M, D), F32), v((2, 8, 32, D), BF), v((2, 8, 32, D), BF), v((2, 8, 32, D), BF),
        v((2, 8, 32, D), BF), v((2, 8, 32, D), BF), v(block, BF), v(block, BF),
        v((2, 64, D), BF), v((64, D), BF), v((16, 8, D), BF), v((16, 8, D), BF),
        v((16, 8, 640), F32), v((16, 8, 640), F32), v((16, 8, 640), F32),
        v((2, 8, 640), F32), v((8, 8, 640), F32), v((8, 640), F32),
        sem((2,)), sem((2,)), sem((3,)), sem((3,)), sem((16,)), sem((16,)), sem((16,)), sem((16,)),
        sem((9,)), sem((9,)), sem((9,)), sem((8,)), sem((8,)), sem((2,)), sem((2,)),
        sem((8,)), sem((8,)), sem((2,)), sem((9,)), sem((9,)),
        sem((16,)), sem((16,)), sem((8,)), sem((8,)), sem((16,)), sem((16,)),
    ]
    tg, rg, wig, wog = pl.pallas_call(
        kernel,
        out_shape=(
            jax.ShapeDtypeStruct((M, D), BF),
            jax.ShapeDtypeStruct((E, D), F32),
            jax.ShapeDtypeStruct((2, D, FS), BF),
            jax.ShapeDtypeStruct((2, FS, D), BF),
        ),
        in_specs=[vm, vm, vm, anyspace, anyspace],
        out_specs=(vm, vm, anyspace, anyspace),
        scratch_shapes=scratch,
        compiler_params=pltpu.CompilerParams(
            collective_id=0, has_side_effects=True, vmem_limit_bytes=56 * 2**20
        ),
        cost_estimate=pl.CostEstimate(
            flops=5 * 10**9, bytes_accessed=13 * 2**20, transcendentals=10**6
        ),
        name="moe_backward",
    )(tokens, out_grad, router, w_in, w_out)
    return tg, rg.T, wig, wog


def solution(mesh):
    both = ("dp", "expert")
    return jax.shard_map(
        local,
        mesh=mesh,
        in_specs=(
            P(both, None), P(), P("expert", None, "dp"), P("expert", "dp", None), P(both, None),
        ),
        out_specs=(P(both, None), P(), P("expert", None, "dp"), P("expert", "dp", None)),
        check_vma=False,
    )
```

```python
import math

import jax
import jax.numpy as jnp
from jax import lax
from jax.experimental import pallas as pl
from jax.experimental.pallas import tpu as pltpu
from jax.sharding import PartitionSpec as P

MESH = pl.DeviceIdType.MESH
M, D, E, FS = 256, 1280, 64, 512
BF, F32 = jnp.bfloat16, jnp.float32
GELU_C, GELU_A = math.sqrt(2.0 / math.pi), 0.044715


def dot(a, b, ca=1, cb=0):
    return lax.dot_general(a, b, (((ca,), (cb,)), ((), ())), preferred_element_type=F32)


def perm(source, inverse):
    rows = lax.broadcasted_iota(jnp.int32, (64, 64), 1 if inverse else 0)
    cols = lax.broadcasted_iota(jnp.int32, (64, 64), 0 if inverse else 1)
    return (source(rows) == cols).astype(F32).astype(BF)


def reorder(matrix, rows):
    return dot(matrix, rows).astype(BF)


def kernel(
    x_hbm, g_hbm, r_hbm, wi_hbm, wo_hbm,
    tg_ref, rg_ref, wig_hbm, wog_hbm,
    x_ref, g_ref, r_ref, wi, wo, wig, wog,
    comb_v, disp_v,
    zs, zr, sv, rv, ob, rows, act, slope_v, hgv,
    p32, cs, cr, pv, rbuf, fo, zs2, zr2, sv2, rv2,
    ra, rb, rc, zb, rf,
    wsem, osem, core_s, core_r, xs1, xr1, xs2, xr2,
    gr, gsu, gcs, gcr, pcs, pcr,
    rur, rsu, as1, ar1, az_s, az_r, as2, ar2,
):
    dp, ex = lax.axis_index("dp"), lax.axis_index("expert")
    c, q = dp % 2, dp // 2
    h, xy = ex // 16, ex % 16
    y, x = xy // 4, xy % 4
    z = h * 4 + q

    loads = [
        pltpu.make_async_copy(src, dst, wsem.at[k])
        for k, (src, dst) in enumerate(
            [(x_hbm, x_ref), (r_hbm, r_ref), (g_hbm, g_ref), (wi_hbm, wi), (wo_hbm, wo)]
        )
    ]
    for cp in loads:
        cp.start()

    core_peer = (q * 2 + (1 - c), ex)
    xy_peers = []
    for d in (10, 2, 8, 11, 9, 14, 6, 15, 13, 7, 5, 3, 1, 12, 4):
        to = ((y + d // 4) % 4) * 4 + (x + d % 4) % 4
        xy_peers.append((d, to))

    def z_dev(hh, qq):
        return (qq * 2 + c, hh * 16 + xy)

    barrier = pltpu.get_barrier_semaphore()

    def greet(dev):
        pl.semaphore_signal(barrier, inc=1, device_id=dev, device_id_type=MESH)

    for d, to in xy_peers:
        greet((dp, h * 16 + to))
    z_peers = []
    for d in (9, 8, 7, 11, 6, 10, 5, 13, 4, 12, 3, 15, 2, 14, 1):
        zt, ct = (z + d // 2) % 8, (c + d % 2) % 2
        frm = ((z + 8 - d // 2) % 8) * 2 + ct
        z_peers.append((d, (zt % 4 * 2 + ct, zt // 4 * 16 + xy), frm))
        greet(z_peers[-1][1])

    def remote(src, dst, ss, rs, dev):
        return pltpu.make_async_remote_copy(
            src_ref=src, dst_ref=dst, send_sem=ss, recv_sem=rs, device_id=dev, device_id_type=MESH
        )

    def order1(r):
        return (r & 31) * 2 + jnp.where(r < 32, c, 1 - c)

    def order2(r):
        half = jnp.where(((r >> 1) & 1) == 0, h, 1 - h)
        return (r & 1) * 32 + half * 16 + (r >> 2)

    def order3(r):
        return ((r >> 1) & 15) * 4 + (r >> 5) * 2 + (r & 1)

    def swap(t):
        return remote(zs.at[t, 1], zr.at[t], core_s.at[t], core_r.at[t], core_peer)

    def swap2(t):
        return remote(zs2.at[t, 1], zr2.at[t], core_s.at[2 + t], core_r.at[2 + t], core_peer)

    def plane_exchange(src, dst, ss, rs, start):
        copies = []
        for d, to in xy_peers:
            cp = remote(src.at[to], dst.at[xy], ss.at[d], rs.at[d], (dp, h * 16 + to))
            if start:
                cp.start()
            copies.append(cp)
        if start:
            dst[xy] = src[xy]
        return copies

    def finish(copies):
        for cp in copies:
            cp.wait()

    def split(t, local_rows):
        zs[t] = reorder(perm(order1, False), local_rows).reshape(2, 32, D)

    def scatter(t):
        swap(t).wait()
        out = reorder(perm(order2, False), jnp.concatenate([zs[t, 0], zr[t]], axis=0))
        for k in range(16):
            sv[t, k] = out[k * 4 : k * 4 + 4]
        return plane_exchange(sv.at[t], rv.at[t], xs1.at[t], xr1.at[t], True)

    def placed(t, copies):
        finish(copies)
        got = jnp.concatenate([rv[t, k] for k in range(16)], axis=0)
        block = reorder(perm(order3, False), got)
        rows[1, t, q] = block[:32]
        ob[t] = block[32:]

    loads[0].wait()
    loads[1].wait()
    logits = dot(x_ref[...], r_ref[...], 1, 1)
    ed = jnp.exp(logits - jnp.max(logits, axis=0, keepdims=True))
    dispatch = ed / jnp.sum(ed, axis=0, keepdims=True)
    disp_v[...] = dispatch
    split(0, dot(dispatch.astype(BF), x_ref[...], 0, 0).astype(BF))
    pl.semaphore_wait(barrier, 30)
    swap(0).start()
    ec = jnp.exp(logits - jnp.max(logits, axis=1, keepdims=True))
    combine = ec / jnp.sum(ec, axis=1, keepdims=True)
    comb_v[...] = combine
    plane0 = scatter(0)
    loads[2].wait()
    split(1, dot(combine.astype(BF), g_ref[...], 0, 0).astype(BF))
    swap(1).start()
    placed(0, plane0)

    G_BEGIN = [
        [("out", 1, 3), ("out", 1, 1), ("own", 0, 2), ("own", 0, 1)],
        [("out", 1, 3), ("own", 0, 3), ("own", 0, 0), ("own", 0, 2)],
        [("out", 1, 0), ("own", 0, 0), ("own", 0, 3), ("own", 0, 1)],
        [("out", 1, 0), ("out", 1, 2), ("own", 0, 1), ("own", 0, 2)],
    ]
    G_EVENTS = [
        [(7, (1,)), (6, (1, 2)), (1, ()), (2, ()), (3, ()), (4, ()), (5, ())],
        [(3, (0,)), (4, (0,)), (0, ()), (2, ()), (5, (0,)), (7, ()), (6, ())],
        [(0, (3,)), (7, (3,)), (3, ()), (1, ()), (6, (3,)), (4, ()), (5, ())],
        [(4, (2,)), (5, (1, 2)), (2, ()), (1, ()), (0, ()), (7, ()), (6, ())],
    ]
    G_SENDS = [
        G_BEGIN[k] + [(idx, 0, to) for idx, targets in G_EVENTS[k] for to in targets] for k in range(4)
    ]

    def on_plane(body):
        for qq in range(4):
            pl.when(q == qq)(lambda qq=qq: body(qq))

    def place(other, qq):
        return z_dev(1 - h if other else h, qq)

    def g_send(t, qq, k):
        kind, other, to = G_SENDS[qq][k]
        idx = qq if kind == "own" else 4 + qq if kind == "out" else kind
        src = ob.at[t] if kind == "out" else rows.at[1, t, idx]
        return remote(src, rows.at[1, t, idx], gsu.at[t, k], gr.at[t, idx], place(other, to))

    def to_core(t, idx):
        return remote(rows.at[1, t, idx], rows.at[0, t, idx], gcs.at[t, idx], gcr.at[t, idx], core_peer)

    def g_begin(t, qq):
        for k in range(len(G_BEGIN[qq])):
            g_send(t, qq, k).start()
        to_core(t, qq).start()

    def g_events(t, first, last):
        def body(qq):
            k = len(G_BEGIN[qq])
            for n, (idx, targets) in enumerate(G_EVENTS[qq]):
                if first <= n < last:
                    dst = rows.at[1, t, idx]
                    remote(dst, dst, gsu.at[t, 0], gr.at[t, idx], core_peer).wait_recv()
                    for _ in targets:
                        g_send(t, qq, k).start()
                        k += 1
                    to_core(t, idx).start()
                else:
                    k += len(targets)

        on_plane(body)

    def g_sent(t, qq):
        for k in range(len(G_SENDS[qq])):
            g_send(t, qq, k).wait_send()

    on_plane(lambda qq: g_begin(0, qq))
    placed(1, scatter(1))
    g_events(0, 0, 2)
    on_plane(lambda qq: g_begin(1, qq))
    g_events(0, 2, 5)
    g_events(1, 0, 2)
    g_events(0, 5, 7)

    loads[3].wait()
    loads[4].wait()

    def core_sum(t):
        return remote(cs.at[t], cr.at[t], pcs.at[t], pcr.at[t], core_peer)

    def keep_sum(t):
        core_sum(t).wait()
        pv[t] = (p32[...] + cr[t].reshape(M, D).astype(F32)).astype(BF).reshape(8, 32, D)

    def forward(s):
        e = c if s == 1 else 1 - c
        hidden = dot(rows[s, 0].reshape(M, D), wi[e])
        inner = jnp.tanh(GELU_C * (hidden + GELU_A * hidden * hidden * hidden))
        cdf = 0.5 * (1.0 + inner)
        slope_v[s] = cdf + hidden * (
            0.5 * (1.0 - inner * inner) * (GELU_C * (1.0 + 3.0 * GELU_A * hidden * hidden))
        )
        active = (hidden * cdf).astype(BF)
        act[s] = active
        return dot(active, wo[e])

    def give_sum(t, value):
        cs[t] = value.astype(BF).reshape(8, 32, D)
        core_sum(t).start()

    p32[...] = forward(1)
    g_events(1, 2, 4)
    for k in range(8):
        to_core(0, k).wait()
    give_sum(0, forward(0))
    keep_sum(0)

    R_BEGIN = [
        [(5, 0, 1), (4, 0, 1), (3, 0, 1), (2, 0, 2), (1, 0, 1)],
        [(6, 0, 0), (7, 0, 0), (0, 0, 0), (2, 0, 2)],
        [(5, 0, 3), (4, 0, 3), (3, 0, 3), (1, 0, 1)],
        [(6, 0, 2), (7, 0, 2), (0, 0, 2), (1, 0, 1), (2, 0, 2)],
    ]
    R_STEPS = [
        [(7, 1, 3, (1,)), (6, 1, 2, (1, 2))],
        [(5, 0, 3, (0,)), (4, 1, 0, (0,)), (3, 0, 3, (0,))],
        [(6, 0, 0, (3,)), (7, 1, 3, (3,)), (0, 0, 0, (3,))],
        [(4, 1, 0, (2,)), (5, 1, 1, (2, 1))],
    ]
    R_SLOTS = [
        [(7, 1), (6, 1), (6, 2), (0, 1), (0, 2), ("o", 3), ("o", 1)],
        [(5, 0), (4, 0), (3, 0), (1, 0), (1, 2), (1, 3), ("o", 3)],
        [(6, 3), (7, 3), (0, 3), (2, 3), (2, 1), (2, 0), ("o", 0)],
        [(4, 2), (5, 2), (5, 1), (3, 2), (3, 1), ("o", 0), ("o", 2)],
    ]

    def r_send(t, qq, k):
        begin = R_BEGIN[qq]
        if k < len(begin):
            idx, other, to = begin[k]
            src = pv.at[t, idx]
        else:
            idx, other, to, parts = R_STEPS[qq][k - len(begin)]
            src = rbuf.at[t, R_SLOTS[qq].index((idx, parts[0]))]
        slot = R_SLOTS[to].index(("o" if other else idx, qq))
        return remote(src, rbuf.at[t, slot], rsu.at[t, k], rur.at[t, slot], place(other, to))

    def r_wait(t, qq, key):
        slot = R_SLOTS[qq].index(key)
        dst = rbuf.at[t, slot]
        remote(dst, dst, rsu.at[t, 0], rur.at[t, slot], core_peer).wait_recv()
        return slot

    def r_begin(t, qq):
        for k in range(len(R_BEGIN[qq])):
            r_send(t, qq, k).start()

    def r_steps(t, first, last):
        def body(qq):
            for n, (idx, other, to, parts) in list(enumerate(R_STEPS[qq]))[first:last]:
                total = pv[t, idx].astype(F32)
                slots = [r_wait(t, qq, (idx, p)) for p in parts]
                for slot in slots:
                    total = total + rbuf[t, slot].astype(F32)
                rbuf[t, slots[0]] = total.astype(BF)
                r_send(t, qq, len(R_BEGIN[qq]) + n).start()

        on_plane(body)

    def r_sent(t, qq):
        for k in range(len(R_BEGIN[qq]) + len(R_STEPS[qq])):
            r_send(t, qq, k).wait_send()

    def r_total(t, qq):
        total = pv[t, qq].astype(F32)
        outer = None
        for idx, p in R_SLOTS[qq]:
            if idx in (qq, "o"):
                value = rbuf[t, r_wait(t, qq, (idx, p))].astype(F32)
                if idx == qq:
                    total = total + value
                else:
                    outer = value if outer is None else outer + value
        zs2[t, 0] = total.astype(BF)
        fo[t] = outer.astype(BF)

    on_plane(lambda qq: r_begin(0, qq))
    g_events(1, 4, 7)
    for k in range(8):
        to_core(1, k).wait()

    def backward(s):
        e = c if s == 1 else 1 - c
        hg = (dot(rows[s, 1].reshape(M, D), wo[e], 1, 1) * slope_v[s]).astype(BF)
        hgv[s] = hg
        return dot(hg, wi[e], 1, 1)

    p32[...] = backward(1)
    r_steps(0, 0, 1)
    give_sum(1, backward(0))
    r_steps(0, 1, 3)
    keep_sum(1)
    on_plane(lambda qq: r_begin(1, qq))

    def w_out_grad(s, _):
        wog[jnp.where(s == 1, c, 1 - c)] = dot(act[s], rows[s, 1].reshape(M, D), 0, 0).astype(BF)
        return 0

    lax.fori_loop(0, 2, w_out_grad, 0)

    def gathered_back(t):
        both = jnp.concatenate([zs2[t, 0], fo[t]], axis=0)
        out = reorder(perm(order3, True), both)
        for k in range(16):
            sv2[t, k] = out[k * 4 : k * 4 + 4]
        return plane_exchange(sv2.at[t], rv2.at[t], xs2.at[t], xr2.at[t], True)

    def swap_back(t, copies):
        finish(copies)
        got = jnp.concatenate([rv2[t, k] for k in range(16)], axis=0)
        zs2[t] = reorder(perm(order2, True), got).reshape(2, 32, D)
        swap2(t).start()

    def image_rows(t):
        swap2(t).wait()
        return reorder(perm(order1, True), jnp.concatenate([zs2[t, 0], zr2[t]], axis=0))

    on_plane(lambda qq: r_total(0, qq))
    back0 = gathered_back(0)

    r_steps(1, 0, 3)
    swap_back(0, back0)

    def w_in_grad(s, _):
        wig[jnp.where(s == 1, c, 1 - c)] = dot(rows[s, 0].reshape(M, D), hgv[s], 0, 0).astype(BF)
        return 0

    out_copies = [
        pltpu.make_async_copy(wig, wig_hbm, osem.at[0]),
        pltpu.make_async_copy(wog, wog_hbm, osem.at[1]),
    ]
    on_plane(lambda qq: r_total(1, qq))
    back1 = gathered_back(1)
    lax.fori_loop(0, 2, w_in_grad, 0)
    for cp in out_copies:
        cp.start()
    slot_out = image_rows(0)
    cg = dot(g_ref[...], slot_out, 1, 1)
    combine, dispatch = comb_v[...], disp_v[...]
    lg = combine * (cg - jnp.sum(cg * combine, axis=1, keepdims=True))
    swap_back(1, back1)
    slot_in = image_rows(1)

    dg = dot(x_ref[...], slot_in, 1, 1)
    lg = lg + dispatch * (dg - jnp.sum(dg * dispatch, axis=0, keepdims=True))
    lb = lg.astype(BF)
    part = dot(lb, x_ref[...], 0, 0)
    for p in range(16):
        ra[p] = part[p // 2 * 8 : p // 2 * 8 + 8, p % 2 * 640 : p % 2 * 640 + 640].astype(BF)
    copies = plane_exchange(ra, rb, as1, ar1, True)
    tg_ref[...] = (dot(dispatch.astype(BF), slot_in) + dot(lb, r_ref[...])).astype(BF)

    def all_sent(qq):
        for t in range(2):
            g_sent(t, qq)
            r_sent(t, qq)

    on_plane(all_sent)
    finish(copies)
    total = rb[0].astype(F32)
    for p in range(1, 16):
        total = total + rb[p].astype(F32)
    me = z * 2 + c
    zb[me] = total.astype(BF)
    copies = []
    for d, dev, frm in z_peers:
        cp = remote(zb.at[me], zb.at[me], az_s.at[d], az_r.at[d], dev)
        cp.start()
        copies.append((cp, remote(zb.at[frm], zb.at[frm], az_s.at[d], az_r.at[d], dev)))
    for sent, got in copies:
        sent.wait_send()
        got.wait_recv()
    total = zb[0].astype(F32)
    for p in range(1, 16):
        total = total + zb[p].astype(F32)
    rf[...] = total.astype(BF)
    rc[xy] = total.astype(BF)
    copies = []
    for d, to in xy_peers:
        cp = remote(rf, rc.at[xy], as2.at[d], ar2.at[d], (dp, h * 16 + to))
        cp.start()
        copies.append(cp)
    finish(copies)
    rg_ref[...] = rc[...]
    for cp in out_copies:
        cp.wait()


def deliver(tg, rg, wig, wog, tg_out, rg_out, wig_out, wog_out, sem):
    copies = [pltpu.make_async_copy(tg, tg_out, sem.at[8])]
    for k in range(2):
        for half in range(2):
            part = pl.ds(half * (D // 2), D // 2)
            copies.append(pltpu.make_async_copy(wig.at[k, part], wig_out.at[k, part], sem.at[k * 2 + half]))
            part = pl.ds(half * (FS // 2), FS // 2)
            copies.append(
                pltpu.make_async_copy(wog.at[k, part], wog_out.at[k, part], sem.at[4 + k * 2 + half])
            )
    for cp in copies:
        cp.start()
    for p in range(16):
        rg_out[p // 2 * 8 : p // 2 * 8 + 8, p % 2 * 640 : p % 2 * 640 + 640] = rg[p].astype(F32)
    for cp in copies:
        cp.wait()


def local(tokens, router, w_in, w_out, out_grad):
    vm = pl.BlockSpec(memory_space=pltpu.VMEM)
    anyspace = pl.BlockSpec(memory_space=pl.ANY)
    sem = pltpu.SemaphoreType.DMA
    v = pltpu.VMEM
    block, line = (2, 32, D), (2, 8, 32, D)
    scratch = [
        v((M, D), BF), v((M, D), BF), v((E, D), BF),
        v((2, D, FS), BF), v((2, FS, D), BF), v((2, D, FS), BF), v((2, FS, D), BF),
        v((M, E), F32), v((M, E), F32),
        v((2, 2, 32, D), BF), v(block, BF), v((2, 16, 4, D), BF), v((2, 16, 4, D), BF),
        v(block, BF), v((2, 2, 8, 32, D), BF),
        v((2, M, FS), BF), v((2, M, FS), F32), v((2, M, FS), BF),
        v((M, D), F32), v(line, BF), v(line, BF), v(line, BF), v((2, 7, 32, D), BF), v(block, BF),
        v((2, 2, 32, D), BF), v(block, BF), v((2, 16, 4, D), BF), v((2, 16, 4, D), BF),
        v((16, 8, 640), BF), v((16, 8, 640), BF), v((16, 8, 640), BF),
        v((16, 8, 640), BF), v((8, 640), BF),
        sem((5,)), sem((2,)), sem((4,)), sem((4,)),
        sem((2, 16)), sem((2, 16)), sem((2, 16)), sem((2, 16)),
        sem((2, 8)), sem((2, 7)), sem((2, 8)), sem((2, 8)), sem((2,)), sem((2,)),
        sem((2, 7)), sem((2, 7)),
        sem((16,)), sem((16,)), sem((16,)), sem((16,)), sem((16,)), sem((16,)),
    ]
    tg, rg, wig, wog = pl.pallas_call(
        kernel,
        out_shape=(
            jax.ShapeDtypeStruct((M, D), BF),
            jax.ShapeDtypeStruct((16, 8, 640), BF),
            jax.ShapeDtypeStruct((2, D, FS), BF),
            jax.ShapeDtypeStruct((2, FS, D), BF),
        ),
        in_specs=[pl.BlockSpec(memory_space=pltpu.HBM)] * 5,
        out_specs=(vm, vm, anyspace, anyspace),
        scratch_shapes=scratch,
        compiler_params=pltpu.CompilerParams(
            collective_id=0, has_side_effects=True, vmem_limit_bytes=46 * 2**20
        ),
        cost_estimate=pl.CostEstimate(
            flops=5 * 10**9, bytes_accessed=13 * 2**20, transcendentals=10**6
        ),
        name="moe_backward",
    )(tokens, out_grad, router.T, w_in, w_out)
    outs = pl.pallas_call(
        deliver,
        out_shape=(
            jax.ShapeDtypeStruct((M, D), BF),
            jax.ShapeDtypeStruct((E, D), F32),
            jax.ShapeDtypeStruct((2, D, FS), BF),
            jax.ShapeDtypeStruct((2, FS, D), BF),
        ),
        in_specs=[anyspace, vm, anyspace, anyspace],
        out_specs=(anyspace, vm, anyspace, anyspace),
        scratch_shapes=[sem((9,))],
        compiler_params=pltpu.CompilerParams(vmem_limit_bytes=4 * 2**20),
        cost_estimate=pl.CostEstimate(flops=0, bytes_accessed=12 * 2**20, transcendentals=0),
        name="deliver",
    )(tg, rg, wig, wog)
    return outs[0], outs[1].T, outs[2], outs[3]


def solution(mesh):
    both = ("dp", "expert")
    return jax.shard_map(
        local,
        mesh=mesh,
        in_specs=(
            P(both, None), P(), P("expert", None, "dp"), P("expert", "dp", None), P(both, None),
        ),
        out_specs=(P(both, None), P(), P("expert", None, "dp"), P("expert", "dp", None)),
        check_vma=False,
    )
```

```python
import math

import jax
import jax.numpy as jnp
from jax import lax
from jax.experimental import pallas as pl
from jax.experimental.pallas import tpu as pltpu
from jax.sharding import PartitionSpec as P

MESH = pl.DeviceIdType.MESH
M, D, E, FS = 256, 1280, 64, 512
BF, F32 = jnp.bfloat16, jnp.float32
GELU_C, GELU_A = math.sqrt(2.0 / math.pi), 0.044715


def dot(a, b, ca=1, cb=0):
    return lax.dot_general(a, b, (((ca,), (cb,)), ((), ())), preferred_element_type=F32)


def perm(source, inverse):
    rows = lax.broadcasted_iota(jnp.int32, (64, 64), 1 if inverse else 0)
    cols = lax.broadcasted_iota(jnp.int32, (64, 64), 0 if inverse else 1)
    return (source(rows) == cols).astype(F32).astype(BF)


def reorder(matrix, rows):
    return dot(matrix, rows).astype(BF)


def kernel(
    x_hbm, g_hbm, r_hbm, wi_hbm, wo_hbm,
    tg_ref, rg_ref, wig_hbm, wog_hbm,
    x_ref, g_ref, r_ref, wi, wo, wig, wog,
    comb_v, disp_v,
    zs, zr, sv, rv, ob, rows, act, slope_v, hgv,
    p32, cs, cr, pv, rbuf, fo, zs2, zr2, sv2, rv2,
    ra, rb, rc, rp, zb, rf,
    wsem, osem, core_s, core_r, xs1, xr1, xs2, xr2,
    gr, gsu, gcs, gcr, pcs, pcr,
    rur, rsu, as1, ar1, az_s, az_r, as2, ar2,
):
    dp, ex = lax.axis_index("dp"), lax.axis_index("expert")
    c, q = dp % 2, dp // 2
    h, xy = ex // 16, ex % 16
    y, x = xy // 4, xy % 4
    z = h * 4 + q

    loads = [
        pltpu.make_async_copy(src, dst, wsem.at[k])
        for k, (src, dst) in enumerate(
            [(x_hbm, x_ref), (r_hbm, r_ref), (g_hbm, g_ref), (wi_hbm, wi), (wo_hbm, wo)]
        )
    ]
    for cp in loads[:3]:
        cp.start()

    core_peer = (q * 2 + (1 - c), ex)
    xy_peers = []
    for d in (10, 2, 8, 11, 9, 14, 6, 15, 13, 7, 5, 3, 1, 12, 4):
        to = ((y + d // 4) % 4) * 4 + (x + d % 4) % 4
        xy_peers.append((d, to))

    def z_dev(hh, qq):
        return (qq * 2 + c, hh * 16 + xy)

    barrier = pltpu.get_barrier_semaphore()

    def greet(dev):
        pl.semaphore_signal(barrier, inc=1, device_id=dev, device_id_type=MESH)

    for d, to in xy_peers:
        greet((dp, h * 16 + to))
    greet(core_peer)
    z_peers = []
    for d in (4, 3, 5, 2, 6, 1, 7):
        zt = (z + d) % 8
        z_peers.append((d, (zt % 4 * 2 + c, zt // 4 * 16 + xy), (z + 8 - d) % 8))
        greet(z_peers[-1][1])

    def remote(src, dst, ss, rs, dev):
        return pltpu.make_async_remote_copy(
            src_ref=src, dst_ref=dst, send_sem=ss, recv_sem=rs, device_id=dev, device_id_type=MESH
        )

    def order1(r):
        return (r & 31) * 2 + jnp.where(r < 32, c, 1 - c)

    def order2(r):
        half = jnp.where(((r >> 1) & 1) == 0, h, 1 - h)
        return (r & 1) * 32 + half * 16 + (r >> 2)

    def order3(r):
        return ((r >> 1) & 15) * 4 + (r >> 5) * 2 + (r & 1)

    def swap(t):
        return remote(zs.at[t, 1], zr.at[t], core_s.at[t], core_r.at[t], core_peer)

    def swap2(t):
        return remote(zs2.at[t, 1], zr2.at[t], core_s.at[2 + t], core_r.at[2 + t], core_peer)

    def plane_exchange(src, dst, ss, rs, start):
        copies = []
        for d, to in xy_peers:
            cp = remote(src.at[to], dst.at[xy], ss.at[d], rs.at[d], (dp, h * 16 + to))
            if start:
                cp.start()
            copies.append(cp)
        if start:
            dst[xy] = src[xy]
        return copies

    def finish(copies):
        for cp in copies:
            cp.wait()

    def split(t, local_rows):
        zs[t] = reorder(perm(order1, False), local_rows).reshape(2, 32, D)

    def scatter(t):
        swap(t).wait()
        out = reorder(perm(order2, False), jnp.concatenate([zs[t, 0], zr[t]], axis=0))
        for k in range(16):
            sv[t, k] = out[k * 4 : k * 4 + 4]
        return plane_exchange(sv.at[t], rv.at[t], xs1.at[t], xr1.at[t], True)

    def placed(t, copies):
        finish(copies)
        got = jnp.concatenate([rv[t, k] for k in range(16)], axis=0)
        block = reorder(perm(order3, False), got)
        rows[1, t, q] = block[:32]
        ob[t] = block[32:]

    loads[0].wait()
    loads[1].wait()
    for cp in loads[3:]:
        cp.start()
    logits = dot(x_ref[...], r_ref[...], 1, 1)
    ed = jnp.exp(logits - jnp.max(logits, axis=0, keepdims=True))
    dispatch = ed / jnp.sum(ed, axis=0, keepdims=True)
    disp_v[...] = dispatch
    split(0, dot(dispatch.astype(BF), x_ref[...], 0, 0).astype(BF))
    pl.semaphore_wait(barrier, 23)
    swap(0).start()
    ec = jnp.exp(logits - jnp.max(logits, axis=1, keepdims=True))
    combine = ec / jnp.sum(ec, axis=1, keepdims=True)
    comb_v[...] = combine
    plane0 = scatter(0)
    loads[2].wait()
    split(1, dot(combine.astype(BF), g_ref[...], 0, 0).astype(BF))
    swap(1).start()
    placed(0, plane0)

    G_BEGIN = [
        [("out", 1, 3), ("out", 1, 1), ("own", 0, 2), ("own", 0, 1)],
        [("out", 1, 3), ("own", 0, 3), ("own", 0, 0), ("own", 0, 2)],
        [("out", 1, 0), ("own", 0, 0), ("own", 0, 3), ("own", 0, 1)],
        [("out", 1, 0), ("out", 1, 2), ("own", 0, 1), ("own", 0, 2)],
    ]
    G_EVENTS = [
        [(7, (1,)), (6, (1, 2)), (1, ()), (2, ()), (3, ()), (4, ()), (5, ())],
        [(3, (0,)), (4, (0,)), (0, ()), (2, ()), (5, (0,)), (7, ()), (6, ())],
        [(0, (3,)), (7, (3,)), (3, ()), (1, ()), (6, (3,)), (4, ()), (5, ())],
        [(4, (2,)), (5, (1, 2)), (2, ()), (1, ()), (0, ()), (7, ()), (6, ())],
    ]
    G_SENDS = [
        G_BEGIN[k] + [(idx, 0, to) for idx, targets in G_EVENTS[k] for to in targets] for k in range(4)
    ]

    def on_plane(body):
        for qq in range(4):
            pl.when(q == qq)(lambda qq=qq: body(qq))

    def place(other, qq):
        return z_dev(1 - h if other else h, qq)

    def g_send(t, qq, k):
        kind, other, to = G_SENDS[qq][k]
        idx = qq if kind == "own" else 4 + qq if kind == "out" else kind
        src = ob.at[t] if kind == "out" else rows.at[1, t, idx]
        return remote(src, rows.at[1, t, idx], gsu.at[t, k], gr.at[t, idx], place(other, to))

    def to_core(t, idx):
        return remote(rows.at[1, t, idx], rows.at[0, t, idx], gcs.at[t, idx], gcr.at[t, idx], core_peer)

    def g_begin(t, qq):
        for k in range(len(G_BEGIN[qq])):
            g_send(t, qq, k).start()
        to_core(t, qq).start()

    def g_events(t, first, last):
        def body(qq):
            k = len(G_BEGIN[qq])
            for n, (idx, targets) in enumerate(G_EVENTS[qq]):
                if first <= n < last:
                    dst = rows.at[1, t, idx]
                    remote(dst, dst, gsu.at[t, 0], gr.at[t, idx], core_peer).wait_recv()
                    for _ in targets:
                        g_send(t, qq, k).start()
                        k += 1
                    to_core(t, idx).start()
                else:
                    k += len(targets)

        on_plane(body)

    def g_sent(t, qq):
        for k in range(len(G_SENDS[qq])):
            g_send(t, qq, k).wait_send()

    on_plane(lambda qq: g_begin(0, qq))
    placed(1, scatter(1))
    on_plane(lambda qq: g_begin(1, qq))
    g_events(0, 0, 2)
    g_events(0, 2, 5)
    g_events(0, 5, 7)
    g_events(1, 0, 2)

    loads[3].wait()
    loads[4].wait()

    def core_sum(t):
        return remote(cs.at[t], cr.at[t], pcs.at[t], pcr.at[t], core_peer)

    def keep_sum(t):
        core_sum(t).wait()
        pv[t] = (p32[...] + cr[t].reshape(M, D).astype(F32)).astype(BF).reshape(8, 32, D)

    def forward(s):
        e = c if s == 1 else 1 - c
        hidden = dot(rows[s, 0].reshape(M, D), wi[e])
        inner = jnp.tanh(GELU_C * (hidden + GELU_A * hidden * hidden * hidden))
        cdf = 0.5 * (1.0 + inner)
        slope_v[s] = cdf + hidden * (
            0.5 * (1.0 - inner * inner) * (GELU_C * (1.0 + 3.0 * GELU_A * hidden * hidden))
        )
        active = (hidden * cdf).astype(BF)
        act[s] = active
        return dot(active, wo[e])

    def give_sum(t, value):
        cs[t] = value.astype(BF).reshape(8, 32, D)
        core_sum(t).start()

    p32[...] = forward(1)
    g_events(1, 2, 4)
    for k in range(8):
        to_core(0, k).wait()
    give_sum(0, forward(0))
    keep_sum(0)

    R_BEGIN = [
        [(5, 0, 1), (4, 0, 1), (3, 0, 1), (2, 0, 2), (1, 0, 1)],
        [(6, 0, 0), (7, 0, 0), (0, 0, 0), (2, 0, 2)],
        [(5, 0, 3), (4, 0, 3), (3, 0, 3), (1, 0, 1)],
        [(6, 0, 2), (7, 0, 2), (0, 0, 2), (1, 0, 1), (2, 0, 2)],
    ]
    R_STEPS = [
        [(7, 1, 3, (1,)), (6, 1, 2, (1, 2))],
        [(5, 0, 3, (0,)), (4, 1, 0, (0,)), (3, 0, 3, (0,))],
        [(6, 0, 0, (3,)), (7, 1, 3, (3,)), (0, 0, 0, (3,))],
        [(4, 1, 0, (2,)), (5, 1, 1, (2, 1))],
    ]
    R_SLOTS = [
        [(7, 1), (6, 1), (6, 2), (0, 1), (0, 2), ("o", 3), ("o", 1)],
        [(5, 0), (4, 0), (3, 0), (1, 0), (1, 2), (1, 3), ("o", 3)],
        [(6, 3), (7, 3), (0, 3), (2, 3), (2, 1), (2, 0), ("o", 0)],
        [(4, 2), (5, 2), (5, 1), (3, 2), (3, 1), ("o", 0), ("o", 2)],
    ]

    def r_send(t, qq, k):
        begin = R_BEGIN[qq]
        if k < len(begin):
            idx, other, to = begin[k]
            src = pv.at[t, idx]
        else:
            idx, other, to, parts = R_STEPS[qq][k - len(begin)]
            src = rbuf.at[t, R_SLOTS[qq].index((idx, parts[0]))]
        slot = R_SLOTS[to].index(("o" if other else idx, qq))
        return remote(src, rbuf.at[t, slot], rsu.at[t, k], rur.at[t, slot], place(other, to))

    def r_wait(t, qq, key):
        slot = R_SLOTS[qq].index(key)
        dst = rbuf.at[t, slot]
        remote(dst, dst, rsu.at[t, 0], rur.at[t, slot], core_peer).wait_recv()
        return slot

    def r_begin(t, qq):
        for k in range(len(R_BEGIN[qq])):
            r_send(t, qq, k).start()

    def r_steps(t, first, last):
        def body(qq):
            for n, (idx, other, to, parts) in list(enumerate(R_STEPS[qq]))[first:last]:
                total = pv[t, idx].astype(F32)
                slots = [r_wait(t, qq, (idx, p)) for p in parts]
                for slot in slots:
                    total = total + rbuf[t, slot].astype(F32)
                rbuf[t, slots[0]] = total.astype(BF)
                r_send(t, qq, len(R_BEGIN[qq]) + n).start()

        on_plane(body)

    def r_sent(t, qq):
        for k in range(len(R_BEGIN[qq]) + len(R_STEPS[qq])):
            r_send(t, qq, k).wait_send()

    def r_total(t, qq):
        total = pv[t, qq].astype(F32)
        outer = None
        for idx, p in R_SLOTS[qq]:
            if idx in (qq, "o"):
                value = rbuf[t, r_wait(t, qq, (idx, p))].astype(F32)
                if idx == qq:
                    total = total + value
                else:
                    outer = value if outer is None else outer + value
        zs2[t, 0] = total.astype(BF)
        fo[t] = outer.astype(BF)

    on_plane(lambda qq: r_begin(0, qq))
    g_events(1, 4, 7)
    for k in range(8):
        to_core(1, k).wait()

    def backward(s):
        e = c if s == 1 else 1 - c
        hg = (dot(rows[s, 1].reshape(M, D), wo[e], 1, 1) * slope_v[s]).astype(BF)
        hgv[s] = hg
        return dot(hg, wi[e], 1, 1)

    p32[...] = backward(1)
    r_steps(0, 0, 1)
    give_sum(1, backward(0))
    r_steps(0, 1, 3)
    keep_sum(1)
    on_plane(lambda qq: r_begin(1, qq))

    def w_out_grad(s, _):
        wog[jnp.where(s == 1, c, 1 - c)] = dot(act[s], rows[s, 1].reshape(M, D), 0, 0).astype(BF)
        return 0

    lax.fori_loop(0, 2, w_out_grad, 0)

    def gathered_back(t):
        both = jnp.concatenate([zs2[t, 0], fo[t]], axis=0)
        out = reorder(perm(order3, True), both)
        for k in range(16):
            sv2[t, k] = out[k * 4 : k * 4 + 4]
        return plane_exchange(sv2.at[t], rv2.at[t], xs2.at[t], xr2.at[t], True)

    def swap_back(t, copies):
        finish(copies)
        got = jnp.concatenate([rv2[t, k] for k in range(16)], axis=0)
        zs2[t] = reorder(perm(order2, True), got).reshape(2, 32, D)
        swap2(t).start()

    def image_rows(t):
        swap2(t).wait()
        return reorder(perm(order1, True), jnp.concatenate([zs2[t, 0], zr2[t]], axis=0))

    on_plane(lambda qq: r_total(0, qq))
    back0 = gathered_back(0)

    r_steps(1, 0, 3)
    swap_back(0, back0)

    def w_in_grad(s, _):
        wig[jnp.where(s == 1, c, 1 - c)] = dot(rows[s, 0].reshape(M, D), hgv[s], 0, 0).astype(BF)
        return 0

    out_copies = [
        pltpu.make_async_copy(wig, wig_hbm, osem.at[0]),
        pltpu.make_async_copy(wog, wog_hbm, osem.at[1]),
    ]
    on_plane(lambda qq: r_total(1, qq))
    back1 = gathered_back(1)
    lax.fori_loop(0, 2, w_in_grad, 0)
    for cp in out_copies:
        cp.start()
    slot_out = image_rows(0)
    cg = dot(g_ref[...], slot_out, 1, 1)
    combine, dispatch = comb_v[...], disp_v[...]
    lg = combine * (cg - jnp.sum(cg * combine, axis=1, keepdims=True))
    swap_back(1, back1)
    slot_in = image_rows(1)

    dg = dot(x_ref[...], slot_in, 1, 1)
    lg = lg + dispatch * (dg - jnp.sum(dg * dispatch, axis=0, keepdims=True))
    lb = lg.astype(BF)
    part = dot(lb, x_ref[...], 0, 0)
    for p in range(16):
        ra[p] = part[p // 2 * 8 : p // 2 * 8 + 8, p % 2 * 640 : p % 2 * 640 + 640].astype(BF)
    copies = plane_exchange(ra, rb, as1, ar1, True)
    tg_ref[...] = (dot(dispatch.astype(BF), slot_in) + dot(lb, r_ref[...])).astype(BF)

    def all_sent(qq):
        for t in range(2):
            g_sent(t, qq)
            r_sent(t, qq)

    on_plane(all_sent)
    finish(copies)
    total = rb[0].astype(F32)
    for p in range(1, 16):
        total = total + rb[p].astype(F32)
    half_sum = total.astype(BF)
    rp[0] = half_sum
    pair = remote(rp.at[0], rp.at[1], core_s.at[4], core_r.at[4], core_peer)
    pair.start()
    pair.wait()
    zb[z] = (rp[0].astype(F32) + rp[1].astype(F32)).astype(BF)
    copies = []
    for d, dev, frm in z_peers:
        cp = remote(zb.at[z], zb.at[z], az_s.at[d], az_r.at[d], dev)
        cp.start()
        copies.append((cp, remote(zb.at[frm], zb.at[frm], az_s.at[d], az_r.at[d], dev)))
    for sent, got in copies:
        sent.wait_send()
        got.wait_recv()
    total = zb[0].astype(F32)
    for p in range(1, 8):
        total = total + zb[p].astype(F32)
    rf[...] = total.astype(BF)
    rc[xy] = total.astype(BF)
    copies = []
    for d, to in xy_peers:
        cp = remote(rf, rc.at[xy], as2.at[d], ar2.at[d], (dp, h * 16 + to))
        cp.start()
        copies.append(cp)
    finish(copies)
    rg_ref[...] = rc[...]
    for cp in out_copies:
        cp.wait()


def deliver(tg, rg, wig, wog, tg_out, rg_out, wig_out, wog_out, sem):
    copies = [pltpu.make_async_copy(tg, tg_out, sem.at[8])]
    for k in range(2):
        for half in range(2):
            part = pl.ds(half * (D // 2), D // 2)
            copies.append(pltpu.make_async_copy(wig.at[k, part], wig_out.at[k, part], sem.at[k * 2 + half]))
            part = pl.ds(half * (FS // 2), FS // 2)
            copies.append(
                pltpu.make_async_copy(wog.at[k, part], wog_out.at[k, part], sem.at[4 + k * 2 + half])
            )
    for cp in copies:
        cp.start()
    for p in range(16):
        rg_out[p // 2 * 8 : p // 2 * 8 + 8, p % 2 * 640 : p % 2 * 640 + 640] = rg[p].astype(F32)
    for cp in copies:
        cp.wait()


def local(tokens, router, w_in, w_out, out_grad):
    vm = pl.BlockSpec(memory_space=pltpu.VMEM)
    anyspace = pl.BlockSpec(memory_space=pl.ANY)
    sem = pltpu.SemaphoreType.DMA
    v = pltpu.VMEM
    block, line = (2, 32, D), (2, 8, 32, D)
    scratch = [
        v((M, D), BF), v((M, D), BF), v((E, D), BF),
        v((2, D, FS), BF), v((2, FS, D), BF), v((2, D, FS), BF), v((2, FS, D), BF),
        v((M, E), F32), v((M, E), F32),
        v((2, 2, 32, D), BF), v(block, BF), v((2, 16, 4, D), BF), v((2, 16, 4, D), BF),
        v(block, BF), v((2, 2, 8, 32, D), BF),
        v((2, M, FS), BF), v((2, M, FS), F32), v((2, M, FS), BF),
        v((M, D), F32), v(line, BF), v(line, BF), v(line, BF), v((2, 7, 32, D), BF), v(block, BF),
        v((2, 2, 32, D), BF), v(block, BF), v((2, 16, 4, D), BF), v((2, 16, 4, D), BF),
        v((16, 8, 640), BF), v((16, 8, 640), BF), v((16, 8, 640), BF),
        v((2, 8, 640), BF), v((8, 8, 640), BF), v((8, 640), BF),
        sem((5,)), sem((2,)), sem((5,)), sem((5,)),
        sem((2, 16)), sem((2, 16)), sem((2, 16)), sem((2, 16)),
        sem((2, 8)), sem((2, 7)), sem((2, 8)), sem((2, 8)), sem((2,)), sem((2,)),
        sem((2, 7)), sem((2, 7)),
        sem((16,)), sem((16,)), sem((16,)), sem((16,)), sem((16,)), sem((16,)),
    ]
    operands = (tokens, out_grad, router.T, w_in, w_out)
    tg, rg, wig, wog = pl.pallas_call(
        kernel,
        out_shape=(
            jax.ShapeDtypeStruct((M, D), BF),
            jax.ShapeDtypeStruct((16, 8, 640), BF),
            jax.ShapeDtypeStruct((2, D, FS), BF),
            jax.ShapeDtypeStruct((2, FS, D), BF),
        ),
        in_specs=[pl.BlockSpec(memory_space=pltpu.HBM)] * 5,
        out_specs=(vm, vm, anyspace, anyspace),
        scratch_shapes=scratch,
        compiler_params=pltpu.CompilerParams(
            collective_id=0, has_side_effects=True, vmem_limit_bytes=46 * 2**20
        ),
        cost_estimate=pl.CostEstimate(
            flops=5 * 10**9, bytes_accessed=13 * 2**20, transcendentals=10**6
        ),
        name="moe_backward",
    )(*(pltpu.with_memory_space_constraint(a, pltpu.HBM) for a in operands))
    outs = pl.pallas_call(
        deliver,
        out_shape=(
            jax.ShapeDtypeStruct((M, D), BF),
            jax.ShapeDtypeStruct((E, D), F32),
            jax.ShapeDtypeStruct((2, D, FS), BF),
            jax.ShapeDtypeStruct((2, FS, D), BF),
        ),
        in_specs=[anyspace, vm, anyspace, anyspace],
        out_specs=(anyspace, vm, anyspace, anyspace),
        scratch_shapes=[sem((9,))],
        compiler_params=pltpu.CompilerParams(vmem_limit_bytes=4 * 2**20),
        cost_estimate=pl.CostEstimate(flops=0, bytes_accessed=12 * 2**20, transcendentals=0),
        name="deliver",
    )(tg, rg, wig, wog)
    return outs[0], outs[1].T, outs[2], outs[3]


def solution(mesh):
    both = ("dp", "expert")
    return jax.shard_map(
        local,
        mesh=mesh,
        in_specs=(
            P(both, None), P(), P("expert", None, "dp"), P("expert", "dp", None), P(both, None),
        ),
        out_specs=(P(both, None), P(), P("expert", None, "dp"), P("expert", "dp", None)),
        check_vma=False,
    )
```

```python
import math

import jax
import jax.numpy as jnp
from jax import lax
from jax.experimental import pallas as pl
from jax.experimental.pallas import tpu as pltpu
from jax.sharding import PartitionSpec as P

MESH = pl.DeviceIdType.MESH
M, D, E, FS = 256, 1280, 64, 512
BF, F32 = jnp.bfloat16, jnp.float32
GELU_C, GELU_A = math.sqrt(2.0 / math.pi), 0.044715


def dot(a, b, ca=1, cb=0):
    return lax.dot_general(a, b, (((ca,), (cb,)), ((), ())), preferred_element_type=F32)


def perm(source, inverse):
    rows = lax.broadcasted_iota(jnp.int32, (64, 64), 1 if inverse else 0)
    cols = lax.broadcasted_iota(jnp.int32, (64, 64), 0 if inverse else 1)
    return (source(rows) == cols).astype(F32).astype(BF)


def reorder(matrix, rows):
    return dot(matrix, rows).astype(BF)


def kernel(
    x_hbm, g_hbm, r_hbm, wi_hbm, wo_hbm,
    tg_ref, rg_ref, wig_hbm, wog_hbm,
    x_ref, g_ref, r_ref, wi, wo, wig, wog,
    comb_v, disp_v,
    zs, zr, sv, rv, ob, rows, act, slope_v, hgv,
    p32, cs, cr, pv, rbuf, fo, zs2, zr2, sv2, rv2,
    ra, rb, rc, rp, zb, rf,
    wsem, osem, core_s, core_r, xs1, xr1, xs2, xr2,
    gr, gsu, gcs, gcr, pcs, pcr,
    rur, rsu, as1, ar1, az_s, az_r, as2, ar2,
):
    dp, ex = lax.axis_index("dp"), lax.axis_index("expert")
    c, q = dp % 2, dp // 2
    h, xy = ex // 16, ex % 16
    y, x = xy // 4, xy % 4
    z = h * 4 + q

    loads = [
        pltpu.make_async_copy(src, dst, wsem.at[k])
        for k, (src, dst) in enumerate(
            [(x_hbm, x_ref), (r_hbm, r_ref), (g_hbm, g_ref), (wi_hbm, wi), (wo_hbm, wo)]
        )
    ]
    for cp in loads[:3]:
        cp.start()

    core_peer = (q * 2 + (1 - c), ex)
    xy_peers = []
    for d in (10, 2, 8, 11, 9, 14, 6, 15, 13, 7, 5, 3, 1, 12, 4):
        to = ((y + d // 4) % 4) * 4 + (x + d % 4) % 4
        xy_peers.append((d, to))

    def z_dev(hh, qq):
        return (qq * 2 + c, hh * 16 + xy)

    barrier = pltpu.get_barrier_semaphore()

    def greet(dev):
        pl.semaphore_signal(barrier, inc=1, device_id=dev, device_id_type=MESH)

    for d, to in xy_peers:
        greet((dp, h * 16 + to))
    greet(core_peer)
    z_peers = []
    for d in (4, 3, 5, 2, 6, 1, 7):
        zt = (z + d) % 8
        z_peers.append((d, (zt % 4 * 2 + c, zt // 4 * 16 + xy), (z + 8 - d) % 8))
        greet(z_peers[-1][1])

    def remote(src, dst, ss, rs, dev):
        return pltpu.make_async_remote_copy(
            src_ref=src, dst_ref=dst, send_sem=ss, recv_sem=rs, device_id=dev, device_id_type=MESH
        )

    def order1(r):
        return (r & 31) * 2 + jnp.where(r < 32, c, 1 - c)

    def order2(r):
        half = jnp.where(((r >> 1) & 1) == 0, h, 1 - h)
        return (r & 1) * 32 + half * 16 + (r >> 2)

    def order3(r):
        return ((r >> 1) & 15) * 4 + (r >> 5) * 2 + (r & 1)

    def swap(t):
        return remote(zs.at[t, 1], zr.at[t], core_s.at[t], core_r.at[t], core_peer)

    def swap2(t):
        return remote(zs2.at[t, 1], zr2.at[t], core_s.at[2 + t], core_r.at[2 + t], core_peer)

    def plane_exchange(src, dst, ss, rs, start):
        copies = []
        for d, to in xy_peers:
            cp = remote(src.at[to], dst.at[xy], ss.at[d], rs.at[d], (dp, h * 16 + to))
            if start:
                cp.start()
            copies.append(cp)
        if start:
            dst[xy] = src[xy]
        return copies

    def finish(copies):
        for cp in copies:
            cp.wait()

    def split(t, local_rows):
        zs[t] = reorder(perm(order1, False), local_rows).reshape(2, 32, D)

    def scatter(t):
        swap(t).wait()
        out = reorder(perm(order2, False), jnp.concatenate([zs[t, 0], zr[t]], axis=0))
        for k in range(16):
            sv[t, k] = out[k * 4 : k * 4 + 4]
        return plane_exchange(sv.at[t], rv.at[t], xs1.at[t], xr1.at[t], True)

    def placed(t, copies):
        finish(copies)
        got = jnp.concatenate([rv[t, k] for k in range(16)], axis=0)
        block = reorder(perm(order3, False), got)
        rows[1, t, q] = block[:32]
        ob[t] = block[32:]

    loads[0].wait()
    loads[1].wait()
    for cp in loads[3:]:
        cp.start()
    logits = dot(x_ref[...], r_ref[...], 1, 1)
    ed = jnp.exp(logits - jnp.max(logits, axis=0, keepdims=True))
    dispatch = ed / jnp.sum(ed, axis=0, keepdims=True)
    disp_v[...] = dispatch
    split(0, dot(dispatch.astype(BF), x_ref[...], 0, 0).astype(BF))
    pl.semaphore_wait(barrier, 23)
    swap(0).start()
    ec = jnp.exp(logits - jnp.max(logits, axis=1, keepdims=True))
    combine = ec / jnp.sum(ec, axis=1, keepdims=True)
    comb_v[...] = combine
    plane0 = scatter(0)
    loads[2].wait()
    split(1, dot(combine.astype(BF), g_ref[...], 0, 0).astype(BF))
    swap(1).start()
    placed(0, plane0)

    G_BEGIN = [
        [("out", 1, 3), ("out", 1, 1), ("own", 0, 2), ("own", 0, 1)],
        [("out", 1, 3), ("own", 0, 3), ("own", 0, 0), ("own", 0, 2)],
        [("out", 1, 0), ("own", 0, 0), ("own", 0, 3), ("own", 0, 1)],
        [("out", 1, 0), ("out", 1, 2), ("own", 0, 1), ("own", 0, 2)],
    ]
    G_EVENTS = [
        [(7, (1,)), (6, (1, 2)), (1, ()), (2, ()), (3, ()), (4, ()), (5, ())],
        [(3, (0,)), (4, (0,)), (0, ()), (2, ()), (5, (0,)), (7, ()), (6, ())],
        [(0, (3,)), (7, (3,)), (3, ()), (1, ()), (6, (3,)), (4, ()), (5, ())],
        [(4, (2,)), (5, (1, 2)), (2, ()), (1, ()), (0, ()), (7, ()), (6, ())],
    ]
    G_SENDS = [
        G_BEGIN[k] + [(idx, 0, to) for idx, targets in G_EVENTS[k] for to in targets] for k in range(4)
    ]

    def on_plane(body):
        for qq in range(4):
            pl.when(q == qq)(lambda qq=qq: body(qq))

    def place(other, qq):
        return z_dev(1 - h if other else h, qq)

    def g_send(t, qq, k):
        kind, other, to = G_SENDS[qq][k]
        idx = qq if kind == "own" else 4 + qq if kind == "out" else kind
        src = ob.at[t] if kind == "out" else rows.at[1, t, idx]
        return remote(src, rows.at[1, t, idx], gsu.at[t, k], gr.at[t, idx], place(other, to))

    def to_core(t, idx):
        return remote(rows.at[1, t, idx], rows.at[0, t, idx], gcs.at[t, idx], gcr.at[t, idx], core_peer)

    def g_begin(t, qq):
        for k in range(len(G_BEGIN[qq])):
            g_send(t, qq, k).start()
        to_core(t, qq).start()

    def g_events(t, first, last):
        def body(qq):
            k = len(G_BEGIN[qq])
            for n, (idx, targets) in enumerate(G_EVENTS[qq]):
                if first <= n < last:
                    dst = rows.at[1, t, idx]
                    remote(dst, dst, gsu.at[t, 0], gr.at[t, idx], core_peer).wait_recv()
                    for _ in targets:
                        g_send(t, qq, k).start()
                        k += 1
                    to_core(t, idx).start()
                else:
                    k += len(targets)

        on_plane(body)

    def g_sent(t, qq):
        for k in range(len(G_SENDS[qq])):
            g_send(t, qq, k).wait_send()

    on_plane(lambda qq: g_begin(0, qq))
    placed(1, scatter(1))
    on_plane(lambda qq: g_begin(1, qq))
    g_events(0, 0, 2)
    g_events(0, 2, 5)
    g_events(0, 5, 7)
    g_events(1, 0, 2)

    loads[3].wait()
    loads[4].wait()

    def core_sum(t):
        return remote(cs.at[t], cr.at[t], pcs.at[t], pcr.at[t], core_peer)

    def keep_sum(t):
        core_sum(t).wait()
        pv[t] = (p32[...] + cr[t].reshape(M, D).astype(F32)).astype(BF).reshape(8, 32, D)

    def forward(s):
        e = c if s == 1 else 1 - c
        hidden = dot(rows[s, 0].reshape(M, D), wi[e])
        inner = jnp.tanh(GELU_C * (hidden + GELU_A * hidden * hidden * hidden))
        cdf = 0.5 * (1.0 + inner)
        slope_v[s] = cdf + hidden * (
            0.5 * (1.0 - inner * inner) * (GELU_C * (1.0 + 3.0 * GELU_A * hidden * hidden))
        )
        active = (hidden * cdf).astype(BF)
        act[s] = active
        return dot(active, wo[e])

    def give_sum(t, value):
        cs[t] = value.astype(BF).reshape(8, 32, D)
        core_sum(t).start()

    p32[...] = forward(1)
    for k in range(8):
        to_core(0, k).wait()
    give_sum(0, forward(0))
    keep_sum(0)

    R_BEGIN = [
        [(5, 0, 1), (4, 0, 1), (3, 0, 1), (2, 0, 2), (1, 0, 1)],
        [(6, 0, 0), (7, 0, 0), (0, 0, 0), (2, 0, 2)],
        [(5, 0, 3), (4, 0, 3), (3, 0, 3), (1, 0, 1)],
        [(6, 0, 2), (7, 0, 2), (0, 0, 2), (1, 0, 1), (2, 0, 2)],
    ]
    R_STEPS = [
        [(7, 1, 3, (1,)), (6, 1, 2, (1, 2))],
        [(5, 0, 3, (0,)), (4, 1, 0, (0,)), (3, 0, 3, (0,))],
        [(6, 0, 0, (3,)), (7, 1, 3, (3,)), (0, 0, 0, (3,))],
        [(4, 1, 0, (2,)), (5, 1, 1, (2, 1))],
    ]
    R_SLOTS = [
        [(7, 1), (6, 1), (6, 2), (0, 1), (0, 2), ("o", 3), ("o", 1)],
        [(5, 0), (4, 0), (3, 0), (1, 0), (1, 2), (1, 3), ("o", 3)],
        [(6, 3), (7, 3), (0, 3), (2, 3), (2, 1), (2, 0), ("o", 0)],
        [(4, 2), (5, 2), (5, 1), (3, 2), (3, 1), ("o", 0), ("o", 2)],
    ]

    def r_send(t, qq, k):
        begin = R_BEGIN[qq]
        if k < len(begin):
            idx, other, to = begin[k]
            src = pv.at[t, idx]
        else:
            idx, other, to, parts = R_STEPS[qq][k - len(begin)]
            src = rbuf.at[t, R_SLOTS[qq].index((idx, parts[0]))]
        slot = R_SLOTS[to].index(("o" if other else idx, qq))
        return remote(src, rbuf.at[t, slot], rsu.at[t, k], rur.at[t, slot], place(other, to))

    def r_wait(t, qq, key):
        slot = R_SLOTS[qq].index(key)
        dst = rbuf.at[t, slot]
        remote(dst, dst, rsu.at[t, 0], rur.at[t, slot], core_peer).wait_recv()
        return slot

    def r_begin(t, qq):
        for k in range(len(R_BEGIN[qq])):
            r_send(t, qq, k).start()

    def r_steps(t, first, last):
        def body(qq):
            for n, (idx, other, to, parts) in list(enumerate(R_STEPS[qq]))[first:last]:
                total = pv[t, idx].astype(F32)
                slots = [r_wait(t, qq, (idx, p)) for p in parts]
                for slot in slots:
                    total = total + rbuf[t, slot].astype(F32)
                rbuf[t, slots[0]] = total.astype(BF)
                r_send(t, qq, len(R_BEGIN[qq]) + n).start()

        on_plane(body)

    def r_sent(t, qq):
        for k in range(len(R_BEGIN[qq]) + len(R_STEPS[qq])):
            r_send(t, qq, k).wait_send()

    def r_total(t, qq):
        total = pv[t, qq].astype(F32)
        outer = None
        for idx, p in R_SLOTS[qq]:
            if idx in (qq, "o"):
                value = rbuf[t, r_wait(t, qq, (idx, p))].astype(F32)
                if idx == qq:
                    total = total + value
                else:
                    outer = value if outer is None else outer + value
        zs2[t, 0] = total.astype(BF)
        fo[t] = outer.astype(BF)

    on_plane(lambda qq: r_begin(0, qq))
    g_events(1, 2, 7)
    for k in range(8):
        to_core(1, k).wait()

    def backward(s):
        e = c if s == 1 else 1 - c
        hg = (dot(rows[s, 1].reshape(M, D), wo[e], 1, 1) * slope_v[s]).astype(BF)
        hgv[s] = hg
        return dot(hg, wi[e], 1, 1)

    p32[...] = backward(1)
    r_steps(0, 0, 1)
    give_sum(1, backward(0))
    r_steps(0, 1, 3)
    keep_sum(1)
    on_plane(lambda qq: r_begin(1, qq))

    def w_out_grad(s, _):
        wog[jnp.where(s == 1, c, 1 - c)] = dot(act[s], rows[s, 1].reshape(M, D), 0, 0).astype(BF)
        return 0

    lax.fori_loop(0, 2, w_out_grad, 0)

    def gathered_back(t):
        both = jnp.concatenate([zs2[t, 0], fo[t]], axis=0)
        out = reorder(perm(order3, True), both)
        for k in range(16):
            sv2[t, k] = out[k * 4 : k * 4 + 4]
        return plane_exchange(sv2.at[t], rv2.at[t], xs2.at[t], xr2.at[t], True)

    def swap_back(t, copies):
        finish(copies)
        got = jnp.concatenate([rv2[t, k] for k in range(16)], axis=0)
        zs2[t] = reorder(perm(order2, True), got).reshape(2, 32, D)
        swap2(t).start()

    def image_rows(t):
        swap2(t).wait()
        return reorder(perm(order1, True), jnp.concatenate([zs2[t, 0], zr2[t]], axis=0))


    r_steps(1, 0, 3)
    on_plane(lambda qq: r_total(0, qq))
    back0 = gathered_back(0)
    on_plane(lambda qq: r_total(1, qq))
    back1 = gathered_back(1)
    swap_back(0, back0)

    def w_in_grad(s, _):
        wig[jnp.where(s == 1, c, 1 - c)] = dot(rows[s, 0].reshape(M, D), hgv[s], 0, 0).astype(BF)
        return 0

    out_copies = [
        pltpu.make_async_copy(wig, wig_hbm, osem.at[0]),
        pltpu.make_async_copy(wog, wog_hbm, osem.at[1]),
    ]
    lax.fori_loop(0, 2, w_in_grad, 0)
    for cp in out_copies:
        cp.start()
    slot_out = image_rows(0)
    cg = dot(g_ref[...], slot_out, 1, 1)
    combine, dispatch = comb_v[...], disp_v[...]
    lg = combine * (cg - jnp.sum(cg * combine, axis=1, keepdims=True))
    swap_back(1, back1)
    slot_in = image_rows(1)

    dg = dot(x_ref[...], slot_in, 1, 1)
    lg = lg + dispatch * (dg - jnp.sum(dg * dispatch, axis=0, keepdims=True))
    lb = lg.astype(BF)
    part = dot(lb, x_ref[...], 0, 0)
    for p in range(16):
        ra[p] = part[p // 2 * 8 : p // 2 * 8 + 8, p % 2 * 640 : p % 2 * 640 + 640].astype(BF)
    copies = plane_exchange(ra, rb, as1, ar1, True)
    tg_ref[...] = (dot(dispatch.astype(BF), slot_in) + dot(lb, r_ref[...])).astype(BF)

    def all_sent(qq):
        for t in range(2):
            g_sent(t, qq)
            r_sent(t, qq)

    on_plane(all_sent)
    finish(copies)
    total = rb[0].astype(F32)
    for p in range(1, 16):
        total = total + rb[p].astype(F32)
    half_sum = total.astype(BF)
    rp[0] = half_sum
    pair = remote(rp.at[0], rp.at[1], core_s.at[4], core_r.at[4], core_peer)
    pair.start()
    pair.wait()
    zb[z] = (rp[0].astype(F32) + rp[1].astype(F32)).astype(BF)
    copies = []
    for d, dev, frm in z_peers:
        cp = remote(zb.at[z], zb.at[z], az_s.at[d], az_r.at[d], dev)
        cp.start()
        copies.append((cp, remote(zb.at[frm], zb.at[frm], az_s.at[d], az_r.at[d], dev)))
    for sent, got in copies:
        sent.wait_send()
        got.wait_recv()
    total = zb[0].astype(F32)
    for p in range(1, 8):
        total = total + zb[p].astype(F32)
    rf[...] = total.astype(BF)
    rc[xy] = total.astype(BF)
    copies = []
    for d, to in xy_peers:
        cp = remote(rf, rc.at[xy], as2.at[d], ar2.at[d], (dp, h * 16 + to))
        cp.start()
        copies.append(cp)
    finish(copies)
    rg_ref[...] = rc[...]
    for cp in out_copies:
        cp.wait()


def deliver(tg, rg, wig, wog, tg_out, rg_out, wig_out, wog_out, sem):
    copies = [pltpu.make_async_copy(tg, tg_out, sem.at[8])]
    for k in range(2):
        for half in range(2):
            part = pl.ds(half * (D // 2), D // 2)
            copies.append(pltpu.make_async_copy(wig.at[k, part], wig_out.at[k, part], sem.at[k * 2 + half]))
            part = pl.ds(half * (FS // 2), FS // 2)
            copies.append(
                pltpu.make_async_copy(wog.at[k, part], wog_out.at[k, part], sem.at[4 + k * 2 + half])
            )
    for cp in copies:
        cp.start()
    for p in range(16):
        rg_out[p // 2 * 8 : p // 2 * 8 + 8, p % 2 * 640 : p % 2 * 640 + 640] = rg[p].astype(F32)
    for cp in copies:
        cp.wait()


def local(tokens, router, w_in, w_out, out_grad):
    vm = pl.BlockSpec(memory_space=pltpu.VMEM)
    anyspace = pl.BlockSpec(memory_space=pl.ANY)
    sem = pltpu.SemaphoreType.DMA
    v = pltpu.VMEM
    block, line = (2, 32, D), (2, 8, 32, D)
    scratch = [
        v((M, D), BF), v((M, D), BF), v((E, D), BF),
        v((2, D, FS), BF), v((2, FS, D), BF), v((2, D, FS), BF), v((2, FS, D), BF),
        v((M, E), F32), v((M, E), F32),
        v((2, 2, 32, D), BF), v(block, BF), v((2, 16, 4, D), BF), v((2, 16, 4, D), BF),
        v(block, BF), v((2, 2, 8, 32, D), BF),
        v((2, M, FS), BF), v((2, M, FS), F32), v((2, M, FS), BF),
        v((M, D), F32), v(line, BF), v(line, BF), v(line, BF), v((2, 7, 32, D), BF), v(block, BF),
        v((2, 2, 32, D), BF), v(block, BF), v((2, 16, 4, D), BF), v((2, 16, 4, D), BF),
        v((16, 8, 640), BF), v((16, 8, 640), BF), v((16, 8, 640), BF),
        v((2, 8, 640), BF), v((8, 8, 640), BF), v((8, 640), BF),
        sem((5,)), sem((2,)), sem((5,)), sem((5,)),
        sem((2, 16)), sem((2, 16)), sem((2, 16)), sem((2, 16)),
        sem((2, 8)), sem((2, 7)), sem((2, 8)), sem((2, 8)), sem((2,)), sem((2,)),
        sem((2, 7)), sem((2, 7)),
        sem((16,)), sem((16,)), sem((16,)), sem((16,)), sem((16,)), sem((16,)),
    ]
    operands = (tokens, out_grad, router.T, w_in, w_out)
    tg, rg, wig, wog = pl.pallas_call(
        kernel,
        out_shape=(
            jax.ShapeDtypeStruct((M, D), BF),
            jax.ShapeDtypeStruct((16, 8, 640), BF),
            jax.ShapeDtypeStruct((2, D, FS), BF),
            jax.ShapeDtypeStruct((2, FS, D), BF),
        ),
        in_specs=[pl.BlockSpec(memory_space=pltpu.HBM)] * 5,
        out_specs=(vm, vm, anyspace, anyspace),
        scratch_shapes=scratch,
        compiler_params=pltpu.CompilerParams(
            collective_id=0, has_side_effects=True, vmem_limit_bytes=46 * 2**20
        ),
        cost_estimate=pl.CostEstimate(
            flops=5 * 10**9, bytes_accessed=13 * 2**20, transcendentals=10**6
        ),
        name="moe_backward",
    )(*(pltpu.with_memory_space_constraint(a, pltpu.HBM) for a in operands))
    outs = pl.pallas_call(
        deliver,
        out_shape=(
            jax.ShapeDtypeStruct((M, D), BF),
            jax.ShapeDtypeStruct((E, D), F32),
            jax.ShapeDtypeStruct((2, D, FS), BF),
            jax.ShapeDtypeStruct((2, FS, D), BF),
        ),
        in_specs=[anyspace, vm, anyspace, anyspace],
        out_specs=(anyspace, vm, anyspace, anyspace),
        scratch_shapes=[sem((9,))],
        compiler_params=pltpu.CompilerParams(vmem_limit_bytes=4 * 2**20),
        cost_estimate=pl.CostEstimate(flops=0, bytes_accessed=12 * 2**20, transcendentals=0),
        name="deliver",
    )(tg, rg, wig, wog)
    return outs[0], outs[1].T, outs[2], outs[3]


def solution(mesh):
    both = ("dp", "expert")
    return jax.shard_map(
        local,
        mesh=mesh,
        in_specs=(
            P(both, None), P(), P("expert", None, "dp"), P("expert", "dp", None), P(both, None),
        ),
        out_specs=(P(both, None), P(), P("expert", None, "dp"), P("expert", "dp", None)),
        check_vma=False,
    )
```
